32 devices in a mesh: replica: 1, fsdp: 32 (over z, y, x, core).
Axes of the slice: x: 2, y: 2, z: 4, core: 2. Of those that a mesh axis runs over, the one named last changes fastest.
Arguments:
- activations: bfloat16 [1, 4096, 8192], P('replica', 'fsdp'), may hold values from -30 to 30, as said below
- key_cotangent: bfloat16 [1, 4096, 512], P('replica', 'fsdp'), may hold values from -6 to 6
- key_gain: float32 [128], replicated, may hold values from 0.25 to 1.75
- local_weight: float32 [1, 8192, 512], P('replica', 'fsdp'), may hold values from -6 to 6
- global_weight: float32 [8192, 512], P('fsdp', 'replica'), may hold values from -6 to 6
- outer_momentum: float32 [8192, 512], P('fsdp', 'replica'), may hold values from -6 to 6
- late_delta: float32 [8192, 512], P('fsdp', 'replica'), may hold values from -6 to 6
Outputs:
- next_local: float32 [1, 8192, 512], P('replica', 'fsdp')
- next_global: float32 [8192, 512], P('fsdp', 'replica')
- next_momentum: float32 [8192, 512], P('fsdp', 'replica')
- outer_delta: float32 [8192, 512], P('fsdp', 'replica')
The draws below stay inside these ranges and needn't reach their ends.
Inputs may be any that keep to these rules, and one draw needn't show every extreme that they name: The activations are the key projection's normalized inputs, and the scale of each input feature differs from feature to feature (by up to about twentyfold).
All inputs are finite; a program needn't handle non-finite values.
Results may differ from the reference program's by a relative error of at most 0.00083.
Values may be sent and summed in bfloat16 or wider, within the bound.
A program may use at most 64 MiB of HBM per device.

```python
import jax
import jax.numpy as jnp
from jax import lax

D = 8192
HEAD = 128
C = 512
TOKENS = 4096
REPLICAS = 1


def draw_activations(key, part):
    key = jax.random.fold_in(key, 11)
    first, second = jax.random.split(key, 2)
    place = jnp.arange(D, dtype=jnp.float32) / (D - 1)
    column = 0.3 * 10.0 ** place * jnp.exp(jax.random.uniform(second, (D,), jnp.float32, -0.4, 0.4))
    base = jax.random.normal(first, (REPLICAS, TOKENS, D), jnp.float32)
    return (jnp.clip(base, -6.0, 6.0) * column).astype(jnp.bfloat16)


def block_levels(key, shape, cuts, low, largest):
    factor_of, own = 1.0, jax.random.fold_in(key, 6)
    for dim, shards_of in cuts:
        steps = jnp.exp(jax.random.uniform(jax.random.fold_in(own, dim), (shards_of,), jnp.float32, low / len(cuts), largest / len(cuts)))
        factor_of = factor_of * jnp.repeat(steps, shape[dim] // shards_of).reshape([-1 if axis == dim else 1 for axis in range(len(shape))])
    return factor_of


def normal_values(key, shape, scale, most, cuts=(), held_as=jnp.bfloat16):
    entries = jax.random.normal(key, shape, jnp.float32) * scale
    if len(cuts) > 0:
        entries = block_levels(key, shape, cuts, -0.22, 0.18) * entries
    return jnp.clip(entries, min=-most, max=most).astype(held_as)


def setup_inputs(seed: int = 0) -> dict:
    seeds = jax.random.split(jax.random.key(seed), 8)
    return {
        "activations": draw_activations(jax.random.fold_in(seeds[7], 71), 0),
        "key_cotangent": normal_values(seeds[1], (REPLICAS, TOKENS, C), 1.0, 6.0, ((1, 32),)),
        "key_gain": jnp.clip(1.0 + 0.15 * jax.random.normal(seeds[2], (HEAD,), jnp.float32), 0.25, 1.75),
        "local_weight": normal_values(seeds[3], (REPLICAS, D, C), 1.0, 6.0, ((1, 32),), jnp.float32),
        "global_weight": normal_values(seeds[4], (D, C), 1.0, 6.0, ((0, 32),), jnp.float32),
        "outer_momentum": normal_values(seeds[5], (D, C), 0.5, 6.0, ((0, 32),), jnp.float32),
        "late_delta": normal_values(seeds[6], (D, C), 0.5, 6.0, ((0, 32),), jnp.float32),
    }


inner_rate = 0.5
outer_rate = 0.7
keep_rate = 0.9
blend_rate = 0.5
epsilon = 1e-06

def step_replica(feats, cotangent, weight, gain):
    width = feats.shape[1]
    factor = width ** (-0.5)
    hidden = jnp.dot(feats, weight.astype(jnp.bfloat16), preferred_element_type=jnp.float32) * factor
    tokens = hidden.shape[0]
    shaped = hidden.reshape(tokens, -1, HEAD)
    spread = jnp.sqrt(lax.optimization_barrier(jnp.mean(shaped * shaped, axis=-1, keepdims=True)) + epsilon)
    unit = shaped / spread
    slope = cotangent.astype(jnp.float32).reshape(tokens, -1, HEAD) * gain
    key_slope = (slope - unit * lax.optimization_barrier(jnp.mean(slope * unit, axis=-1, keepdims=True))) / spread
    key_slope = key_slope.reshape(tokens, -1).astype(jnp.bfloat16)
    gradient = jnp.dot(feats.T, key_slope, preferred_element_type=jnp.float32) * factor
    grad_scale = jnp.sqrt(jnp.sum(gradient * gradient) / gradient.size + epsilon)
    return weight - inner_rate * gradient / grad_scale

def reference(activations, key_cotangent, key_gain, local_weight, global_weight, outer_momentum, late_delta):
    after_step = lax.map(lambda items: step_replica(items[0], items[1], items[2], key_gain), (activations, key_cotangent, local_weight))
    outer_delta = lax.optimization_barrier(jnp.sum(global_weight[None] - after_step, axis=0)) / REPLICAS
    next_momentum = keep_rate * outer_momentum + late_delta
    next_global = global_weight - outer_rate * (late_delta + keep_rate * next_momentum)
    next_local = blend_rate * next_global[None] + (1.0 - blend_rate) * after_step
    return (next_local, next_global, next_momentum, outer_delta)
```

```python
import functools

import jax
import jax.numpy as jnp
from jax import lax
from jax.experimental import pallas as pl
from jax.experimental.pallas import tpu as pltpu
from jax.sharding import PartitionSpec as P

HEAD = 128

inner_rate = 0.5
outer_rate = 0.7
keep_rate = 0.9
blend_rate = 0.5
epsilon = 1e-06

PLACES = 4


def kernel(
    planes, factor, width,
    x_ref, cot_ref, gain_ref, w_ref,
    grad_ref, sq_ref,
    xa, wsend, wa, cbuf, hsend, hbuf, kt, gsend, gbuf, sw_out, sw_in, s1, s2,
    x_send, x_recv, f_send, f_recv, w_send, w_recv, c_send, c_recv, h_send, h_recv,
    k_send, k_recv, g_send, g_recv, sw_send, sw_recv, s1_send, s1_recv, s2_send, s2_recv,
    own_sem,
):
    me = lax.axis_index("fsdp")
    z, q, c = me // (2 * PLACES), (me // 2) % PLACES, me % 2
    tokens = cot_ref.shape[0]
    rows, columns = w_ref.shape
    half = columns // 2
    pair = 2 * rows

    def place(r):
        y, x = q // 2, q % 2
        if r // 2:
            y = 1 - y
        if r % 2:
            x = 1 - x
        return 2 * y + x

    def at(d, r, e):
        zz = z if d == 0 else lax.rem(z + d, planes)
        cc = 1 - c if e else c
        return {"fsdp": (zz * PLACES + place(r)) * 2 + cc}

    plane_peers = [(0, r, e) for r in range(PLACES) for e in range(2) if (r, e) != (0, 0)]
    line_peers = [(d, 0, e) for d in range(1, planes) for e in range(2)]
    barrier = pltpu.get_barrier_semaphore()
    for peer in plane_peers + line_peers:
        pl.semaphore_signal(barrier, inc=1, device_id=at(*peer))
    wsend[0] = w_ref[:, :half].astype(jnp.bfloat16)
    wsend[1] = w_ref[:, half:].astype(jnp.bfloat16)
    pl.semaphore_wait(barrier, len(plane_peers) + len(line_peers))

    def lane(start, size):
        return pl.ds(pl.multiple_of(start, size), size)

    w_copies = {}
    for d in list(range(1, planes)) + [0]:
        for e in range(2):
            if (d, e) == (0, 0):
                continue
            cc = 1 - c if e else c
            w_copies[d, e] = pltpu.make_async_remote_copy(
                wsend.at[cc], wa.at[z, lane(c * rows, rows), :],
                w_send.at[d, e], w_recv.at[d, e], device_id=at(d, 0, e))
            w_copies[d, e].start()

    x_copies = {}
    for zz in range(planes):
        for r in (3, 1, 2):
            x_copies[r, zz] = pltpu.make_async_remote_copy(
                x_ref.at[:, lane(zz * PLACES * pair + place(r) * pair, pair)],
                xa.at[zz, pl.ds(r * 2 * tokens, tokens), :],
                x_send.at[r, zz], x_recv.at[r, zz], device_id=at(0, r, 0))
            x_copies[r, zz].start()
    own = []
    for zz in range(planes):
        src = x_ref.at[:, lane(zz * PLACES * pair + q * pair, pair)]
        mine = pltpu.make_async_copy(src, xa.at[zz, pl.ds(0, tokens), :], own_sem.at[zz])
        mine.start()
        own.append(mine)
        x_copies[0, zz] = pltpu.make_async_remote_copy(
            src, xa.at[zz, pl.ds(tokens, tokens), :],
            f_send.at[0, zz], f_recv.at[0, zz], device_id=at(0, 0, 1))
        x_copies[0, zz].start()
    cot_copy = pltpu.make_async_remote_copy(
        cot_ref.at[:, lane((1 - c) * half, half)], cbuf, c_send, c_recv, device_id=at(0, 0, 1))
    cot_copy.start()

    wa[z, lane(c * rows, rows), :] = wsend[c]

    f_copies = {}
    for zz in range(planes):
        for r in (1, 2, 3):
            x_copies[r, zz].wait_recv()
            block = xa.at[zz, pl.ds(r * 2 * tokens, tokens), :]
            f_copies[r, zz] = pltpu.make_async_remote_copy(
                block, xa.at[zz, pl.ds((r * 2 + 1) * tokens, tokens), :],
                f_send.at[r, zz], f_recv.at[r, zz], device_id=at(0, 0, 1))
            f_copies[r, zz].start()
    for copy in own:
        copy.wait()
    for zz in range(planes):
        x_copies[0, zz].wait_recv()
    for key in w_copies:
        w_copies[key].wait_recv()

    def partial_hidden(r):
        total = None
        for zz in range(planes):
            term = jnp.dot(xa[zz, r * 2 * tokens:(r + 1) * 2 * tokens, :], wa[zz],
                           preferred_element_type=jnp.float32)
            total = term if total is None else total + term
        return total

    h_copies = []
    for r in (3, 1, 2):
        for zz in range(planes):
            f_copies[r, zz].wait_recv()
        hsend[r - 1] = partial_hidden(r).astype(jnp.bfloat16)
        copy = pltpu.make_async_remote_copy(
            hsend.at[r - 1], hbuf.at[r - 1], h_send.at[r - 1], h_recv.at[r - 1],
            device_id=at(0, r, 0))
        copy.start()
        h_copies.append(copy)
    hidden = partial_hidden(0)
    cot_copy.wait_recv()
    first = jnp.where(c == 0, cot_ref[:, :half].astype(jnp.float32),
                      cot_ref[:, half:].astype(jnp.float32))
    cotangent = jnp.concatenate([first, cbuf[...].astype(jnp.float32)], axis=0)
    gain = gain_ref[...]
    for copy in h_copies:
        copy.wait_recv()
    for i in range(PLACES - 1):
        hidden = hidden + hbuf[i].astype(jnp.float32)
    hidden = hidden * factor
    for h in range(half // HEAD):
        cols = slice(h * HEAD, (h + 1) * HEAD)
        shaped = hidden[:, cols]
        spread = jnp.sqrt(jnp.mean(shaped * shaped, axis=-1, keepdims=True) + epsilon)
        unit = shaped / spread
        slope = cotangent[:, cols] * gain
        key_slope = (slope - unit * jnp.mean(slope * unit, axis=-1, keepdims=True)) / spread
        kt[cols, 0:2 * tokens] = jnp.transpose(key_slope).astype(jnp.bfloat16)

    k_copies = []
    for r in (3, 1, 2):
        copy = pltpu.make_async_remote_copy(
            kt.at[:, pl.ds(0, 2 * tokens)], kt.at[:, pl.ds(r * 2 * tokens, 2 * tokens)],
            k_send.at[r - 1], k_recv.at[r - 1], device_id=at(0, r, 0))
        copy.start()
        k_copies.append(copy)
    for copy in k_copies:
        copy.wait_recv()

    g_copies = []
    for d in list(range(1, planes)):
        zz = lax.rem(z + d, planes)
        gsend[d - 1] = jnp.dot(kt[...], xa[zz], preferred_element_type=jnp.float32).astype(jnp.bfloat16)
        copy = pltpu.make_async_remote_copy(
            gsend.at[d - 1], gbuf.at[d - 1], g_send.at[d - 1], g_recv.at[d - 1],
            device_id=at(d, 0, 0))
        copy.start()
        g_copies.append(copy)
    total = jnp.dot(kt[...], xa[z], preferred_element_type=jnp.float32)
    for i, copy in enumerate(g_copies):
        copy.wait_recv()
        total = total + gbuf[i].astype(jnp.float32)
    total = total * factor

    low, high = total[:, :rows], total[:, rows:]
    sw_out[...] = jnp.where(c == 0, high, low)
    sw_copy = pltpu.make_async_remote_copy(
        sw_out, sw_in, sw_send, sw_recv, device_id=at(0, 0, 1))
    sw_copy.start()
    squares = jnp.sum((total * total).reshape(half // 8, 8, pair), axis=0)
    s1[0] = sum(squares[:, i * 128:(i + 1) * 128] for i in range(pair // 128))
    s1_copies = []
    for r in range(PLACES):
        for e in range(2):
            if (r, e) == (0, 0):
                continue
            i = r * 2 + e
            copy = pltpu.make_async_remote_copy(
                s1.at[0], s1.at[i], s1_send.at[i - 1], s1_recv.at[i - 1], device_id=at(0, r, e))
            copy.start()
            s1_copies.append(copy)
    mine = jnp.transpose(jnp.where(c == 0, low, high))
    for copy in s1_copies:
        copy.wait_recv()
    s2[0] = jnp.sum(s1[...], axis=0)
    s2_copies = []
    for d in range(1, planes):
        copy = pltpu.make_async_remote_copy(
            s2.at[0], s2.at[d], s2_send.at[d - 1], s2_recv.at[d - 1], device_id=at(d, 0, 0))
        copy.start()
        s2_copies.append(copy)
    sw_copy.wait_recv()
    other = jnp.transpose(sw_in[...])
    grad_ref[:, :half] = jnp.where(c == 0, mine, other)
    grad_ref[:, half:] = jnp.where(c == 0, other, mine)
    for copy in s2_copies:
        copy.wait_recv()
    everything = jnp.sum(s2[...], axis=0)
    sq_ref[...] = jnp.broadcast_to(
        jnp.sum(jnp.sum(everything, axis=0, keepdims=True), axis=1, keepdims=True), sq_ref.shape)

    for group in (w_copies, x_copies, f_copies):
        for key in group:
            group[key].wait_send()
    for copy in [cot_copy, sw_copy] + h_copies + k_copies + g_copies + s1_copies + s2_copies:
        copy.wait_send()


def sharded_gradient(feats, cotangent, gain, own_rows, devices):
    tokens, width = feats.shape
    rows, columns = own_rows.shape
    planes = devices // (2 * PLACES)
    half, pair = columns // 2, 2 * rows
    bf16, f32 = jnp.bfloat16, jnp.float32
    dma = pltpu.SemaphoreType.DMA
    vmem = pl.BlockSpec(memory_space=pltpu.VMEM)
    others = PLACES - 1
    gradient, squares = pl.pallas_call(
        functools.partial(kernel, planes, width ** (-0.5), width),
        out_shape=(jax.ShapeDtypeStruct((rows, columns), f32), jax.ShapeDtypeStruct((8, 128), f32)),
        in_specs=[pl.BlockSpec(memory_space=pl.ANY), vmem, vmem, vmem],
        out_specs=(vmem, vmem),
        scratch_shapes=[
            pltpu.VMEM((planes, PLACES * 2 * tokens, pair), bf16),
            pltpu.VMEM((2, rows, half), bf16),
            pltpu.VMEM((planes, pair, half), bf16),
            pltpu.VMEM((tokens, half), bf16),
            pltpu.VMEM((others, 2 * tokens, half), bf16),
            pltpu.VMEM((others, 2 * tokens, half), bf16),
            pltpu.VMEM((half, PLACES * 2 * tokens), bf16),
            pltpu.VMEM((planes - 1, half, pair), bf16),
            pltpu.VMEM((planes - 1, half, pair), bf16),
            pltpu.VMEM((half, rows), f32),
            pltpu.VMEM((half, rows), f32),
            pltpu.VMEM((2 * PLACES, 8, 128), f32),
            pltpu.VMEM((planes, 8, 128), f32),
            dma((PLACES, planes)), dma((PLACES, planes)),
            dma((PLACES, planes)), dma((PLACES, planes)),
            dma((planes, 2)), dma((planes, 2)),
            dma, dma,
            dma((others,)), dma((others,)),
            dma((others,)), dma((others,)),
            dma((planes - 1,)), dma((planes - 1,)),
            dma, dma,
            dma((2 * PLACES - 1,)), dma((2 * PLACES - 1,)),
            dma((planes - 1,)), dma((planes - 1,)),
            dma((planes,)),
        ],
        compiler_params=pltpu.CompilerParams(
            collective_id=0, has_side_effects=True, vmem_limit_bytes=40 * 2**20),
    )(feats, cotangent, gain.reshape(1, HEAD), own_rows)
    return gradient, squares[0, 0]


def shards(
    devices,
    activations, key_cotangent, key_gain, local_weight, global_weight, outer_momentum, late_delta
):
    own_rows = local_weight[0]
    width, columns = activations.shape[2], own_rows.shape[1]
    gradient, squares = sharded_gradient(
        activations[0], key_cotangent[0], key_gain, own_rows, devices)
    grad_scale = jnp.sqrt(squares / (width * columns) + epsilon)
    after_step = own_rows - inner_rate * gradient / grad_scale
    replicas = lax.axis_size("replica")
    whole_global = lax.all_gather(global_weight, "replica", axis=1, tiled=True)
    outer_delta = (
        lax.psum_scatter(whole_global - after_step, "replica", scatter_dimension=1, tiled=True)
        / replicas
    )
    next_momentum = keep_rate * outer_momentum + late_delta
    next_global = global_weight - outer_rate * (late_delta + keep_rate * next_momentum)
    new_rows = lax.all_gather(next_global, "replica", axis=1, tiled=True)
    next_local = blend_rate * new_rows + (1.0 - blend_rate) * after_step
    return (next_local[None], next_global, next_momentum, outer_delta)


def solution(mesh):
    in_specs = (
        P("replica", "fsdp", None),
        P("replica", "fsdp", None),
        P(),
        P("replica", "fsdp", None),
        P("fsdp", "replica"),
        P("fsdp", "replica"),
        P("fsdp", "replica"),
    )
    out_specs = (
        P("replica", "fsdp", None),
        P("fsdp", "replica"),
        P("fsdp", "replica"),
        P("fsdp", "replica"),
    )
    return jax.shard_map(
        functools.partial(shards, mesh.shape["fsdp"]),
        mesh=mesh, in_specs=in_specs, out_specs=out_specs, check_vma=False)
```
